128 devices in a mesh: chan: 32 (over z_hi, y, x), hel: 4 (over z_lo, core).
Axes of the slice: x: 4, y: 4, z: 4 (z_hi: 2, z_lo: 2; z = z_hi * 2 + z_lo), core: 2. Of those that a mesh axis runs over, the one named last changes fastest.
Arguments:
- psi_prev: float32 [12, 4096, 256], P('hel', 'chan'), may hold values from -6 to 6
- psi_cur: float32 [12, 4096, 256], P('hel', 'chan'), may hold values from -6 to 6
- blocks: bfloat16 [12, 32, 8, 8, 128, 128], P('hel', 'chan'), may hold values from -0.015625 to 0.015625
- radial_terms: float32 [8, 256], replicated, may hold values from -4 to 4
- energies: float32 [12, 4096], P('hel', 'chan'), may hold values from -0.6 to 0
- rotation: float32 [12, 4096], P('hel', 'chan'), may hold values from 0 to 1
- coriolis: float32 [12, 4096], P('hel', 'chan'), may hold values from 0.2 to 1
- counts: int32 [12], P('hel'), may hold values from 64 to 4096, as said below
- offsets: int32 [12, 7], P('hel'), may hold values from 1 to 31, as said below
Outputs:
- psi_before: float32 [12, 4096, 256], P('hel', 'chan')
- psi_last: float32 [12, 4096, 256], P('hel', 'chan')
The draws below stay inside these ranges and needn't reach their ends.
Inputs may be any that keep to these rules, and one draw needn't show every extreme that they name: `counts`: counts never rise with helicity; helicity 0 has all 4096 channels and the last helicity has 64. Each row holds 7 distinct offsets; its first three are 1, 16 and 31.
All inputs are finite; a program needn't handle non-finite values.
Results may differ from the reference program's by a relative error of at most 0.0045.
Values may be sent and summed in bfloat16 or wider, within the bound.
No kernel may reach another device: no remote copies, remote signals or barrier semaphores. Data moves between devices by JAX's collectives and lax.ppermute only.
A program may use at most 128 MiB of HBM per device.

```python
import math
import jax
import jax.numpy as jnp
from jax import lax

CB = 128
RAD = 256
LAM = 8
STEPS = 2
NBLK = 32
CHAN = 4096
HEL = 12
HALF = 7


def draw_counts(key, part):
    key = jax.random.fold_in(key, 5)
    drops = jax.random.randint(key, (HEL,), 0, 3 * CHAN // HEL + 1)
    helix = jnp.arange(HEL, dtype=jnp.int32)
    drops = jnp.where(helix == 0, 0, drops)
    levels = CHAN - jnp.cumsum(drops)
    levels = jnp.maximum(levels, CB // 2)
    levels = jnp.where(helix == HEL - 1, CB // 2, levels)
    return levels.astype(jnp.int32)


def draw_offsets(key, part):
    key = jax.random.fold_in(key, 11)
    row_keys = jax.random.split(key, HEL)

    def one_row(row_key):
        shuffled = jax.random.permutation(row_key, NBLK - 4).astype(jnp.int32) + 2
        shuffled = jnp.where(shuffled >= NBLK // 2, shuffled + 1, shuffled)
        fixed_three = jnp.array([1, NBLK // 2, NBLK - 1], dtype=jnp.int32)
        return jnp.concatenate([fixed_three, shuffled[:HALF - 3]])
    return jax.vmap(one_row)(row_keys).astype(jnp.int32)


def level_of(key, dims, cuts, low, largest):
    gain = 1.0
    for position, parts in cuts:
        heights = jax.random.uniform(jax.random.fold_in(jax.random.fold_in(key, 6), position), (parts,), jnp.float32, low / len(cuts), largest / len(cuts))
        gain = gain * jnp.repeat(jnp.exp(heights), dims[position] // parts).reshape((-1,) + (1,) * (len(dims) - 1 - position))
    return gain


def noise(own_key, shape, width, bound, cuts=(), held_as=jnp.bfloat16):
    factor_of = level_of(own_key, shape, cuts, -0.22, 0.18) if cuts else 1.0
    entries = jax.random.normal(own_key, shape, jnp.float32) * width * factor_of
    return jnp.minimum(jnp.maximum(entries, -bound), bound).astype(held_as)


def setup_inputs(seed: int = 0) -> dict:
    streams_of = jax.random.split(jax.random.key(seed), 10)
    return {
        "psi_prev": noise(streams_of[0], (HEL, CHAN, RAD), 1.0, 6.0, ((0, 4), (1, 32)), jnp.float32),
        "psi_cur": noise(streams_of[1], (HEL, CHAN, RAD), 1.0, 6.0, ((0, 4), (1, 32)), jnp.float32),
        "blocks": noise(streams_of[2], (HEL, NBLK, HALF + 1, LAM, CB, CB), 0.001, 0.015625, ((0, 4), (1, 32))),
        "radial_terms": noise(streams_of[3], (LAM, RAD), 1.0, 4.0, (), jnp.float32),
        "energies": jnp.clip(-0.6 + 0.6 * jax.random.uniform(streams_of[4], (HEL, CHAN), jnp.float32) ** level_of(streams_of[4], (HEL, CHAN), ((0, 4), (1, 32)), -0.2, 0.2), -0.6, 0.0),
        "rotation": jnp.clip(1.0 * jax.random.uniform(streams_of[5], (HEL, CHAN), jnp.float32) ** level_of(streams_of[5], (HEL, CHAN), ((0, 4), (1, 32)), -0.2, 0.2), 0.0, 1.0),
        "coriolis": jnp.clip(0.2 + 0.8 * jax.random.uniform(streams_of[6], (HEL, CHAN), jnp.float32) ** level_of(streams_of[6], (HEL, CHAN), ((0, 4), (1, 32)), -0.2, 0.2), 0.2, 1.0),
        "counts": draw_counts(jax.random.fold_in(streams_of[9], 71), 0),
        "offsets": draw_offsets(jax.random.fold_in(streams_of[9], 71), 0),
    }


def kinetic_matrix(points):
    node_count = points + 1
    grid_index = jnp.arange(1, node_count, dtype=jnp.int32)
    row_index = grid_index[:, None]
    col_index = grid_index[None, :]
    distance = row_index - col_index
    summed = row_index + col_index
    nonzero_gap = jnp.where(distance == 0, 1, distance).astype(jnp.float32)
    inverse_gap = 1.0 / jnp.sin(math.pi * nonzero_gap / (2.0 * node_count)) ** 2
    inverse_sum = 1.0 / jnp.sin(math.pi * summed.astype(jnp.float32) / (2.0 * node_count)) ** 2
    parity = (1 - 2 * (jnp.abs(distance) % 2)).astype(jnp.float32)
    diagonal_values = (2.0 * node_count * node_count + 1.0) / 3.0 - 1.0 / jnp.sin(math.pi * grid_index.astype(jnp.float32) / node_count) ** 2
    matrix = jnp.where(distance == 0, diagonal_values[:, None], parity * (inverse_gap - inverse_sum))
    return matrix * (0.25 / (node_count * node_count))


def radial_profiles(points):
    radial_index = jnp.arange(points, dtype=jnp.int32).astype(jnp.float32)
    centrifugal = 0.1 / (1.0 + 8.0 * radial_index / points) ** 2
    beyond = jnp.maximum(radial_index - float((3 * points) // 4), 0.0)
    damping = jnp.exp(-0.002 * beyond * beyond)
    return centrifugal, damping


def reference(psi_prev, psi_cur, blocks, radial_terms, energies, rotation, coriolis, counts, offsets):
    active = (jnp.arange(CHAN, dtype=jnp.int32)[None, :] < counts[:, None]).astype(jnp.float32)[:, :, None]
    kinetic = kinetic_matrix(RAD)
    centrifugal, damping = radial_profiles(RAD)

    def one_helicity(packed):
        blocks_h, half_h, offset_row = packed
        block_values = blocks_h.astype(jnp.float32)
        weighted = (half_h.reshape(NBLK, CB, RAD).astype(jnp.float32)[None] * radial_terms[:, None, None, :]).astype(jnp.bfloat16)
        weighted = weighted.astype(jnp.float32)
        diagonal_term = jnp.einsum('blcd,lbdr->bcr', block_values[:, 0], weighted) + jnp.einsum('bldc,lbdr->bcr', block_values[:, 0], weighted)
        row_ids = jnp.arange(NBLK, dtype=jnp.int32)
        target = (row_ids[:, None] + offset_row[None, :]) % NBLK
        sources = weighted[:, target]
        forward = jnp.einsum('bjlcd,lbjdr->bcr', block_values[:, 1:], sources)
        transposed = jnp.einsum('bjlcd,lbcr->bjdr', block_values[:, 1:], weighted)
        anchor = (row_ids[:, None] - offset_row[None, :] + NBLK) % NBLK
        returned = transposed[anchor, jnp.arange(HALF, dtype=jnp.int32)[None, :]]
        returned = jnp.sum(returned, axis=1)
        return (diagonal_term + forward + returned).reshape(NBLK * CB, RAD)

    def apply(state_field):
        psi_half = state_field.astype(jnp.bfloat16)
        coupling = lax.map(one_helicity, (blocks, psi_half, offsets))
        kinetic_term = jnp.dot(state_field.reshape(-1, RAD), kinetic, precision=lax.Precision.HIGHEST, preferred_element_type=jnp.float32).reshape(state_field.shape)
        zero_slab = jnp.zeros((1, CHAN, RAD), jnp.float32)
        above_field = jnp.concatenate([state_field[1:], zero_slab], axis=0)
        below_term = jnp.concatenate([zero_slab, coriolis[:-1, :, None] * state_field[:-1]], axis=0)
        summed = kinetic_term + (energies[:, :, None] + centrifugal * rotation[:, :, None]) * state_field + coupling
        summed = summed - centrifugal * (coriolis[:, :, None] * above_field + below_term)
        return active * summed

    previous = active * psi_prev
    current = active * psi_cur
    for iteration in range(STEPS):
        renewed = damping * (2.0 * apply(current) - damping * previous)
        previous = current
        current = renewed
    return previous, current
```

```python
import functools

import jax
import jax.numpy as jnp
import numpy as np
from jax import lax
from jax.experimental import pallas as pl
from jax.experimental.pallas import tpu as pltpu
from jax.sharding import PartitionSpec as P

STEPS = 2
BF = jnp.bfloat16
F32 = jnp.float32
VMEM_LIMIT = 40 * 1024 * 1024
ROUTED = (0, 1, 2, 3, 4, 5, 6)


def kinetic_matrix(points):
    n = points + 1
    i = np.arange(1, n, dtype=np.float64)[:, None]
    k = i.T
    gap = np.where(i == k, 1.0, i - k)
    parity = 1.0 - 2.0 * (np.abs(i - k) % 2)
    off = parity * (1.0 / np.sin(np.pi * gap / (2 * n)) ** 2 - 1.0 / np.sin(np.pi * (i + k) / (2 * n)) ** 2)
    diagonal = (2.0 * n * n + 1.0) / 3.0 - 1.0 / np.sin(np.pi * i / n) ** 2
    return (np.where(i == k, diagonal, off) * (0.25 / (n * n))).astype(np.float32)


def radial_profiles(points, width):
    r = np.arange(points, dtype=np.float64)
    centrifugal = 0.1 / (1.0 + 8.0 * r / points) ** 2
    damping = np.exp(-0.002 * np.maximum(r - 3 * points // 4, 0.0) ** 2)
    spread = lambda v: np.ascontiguousarray(np.broadcast_to(v.astype(np.float32)[:, None], (points, width)))
    return spread(centrifugal), spread(damping)


def dot_nn(a, b):
    return lax.dot_general(a, b, (((1,), (0,)), ((), ())), preferred_element_type=F32)


def dot_nt(a, b):
    return lax.dot_general(a, b, (((1,), (1,)), ((), ())), preferred_element_type=F32)


def active_row(remaining_ref, h, width):
    lane = lax.broadcasted_iota(jnp.int32, (1, width), 1)
    return (lane < remaining_ref[h]).astype(F32)


def radial_column(rt_ref, term, shape):
    return jnp.broadcast_to(rt_ref[:, term : term + 1], shape)


def emit_products(h, field, blocks_ref, rt_ref, pieces_ref):
    points, width = field.shape
    terms = blocks_ref.shape[3]
    half = field.astype(BF)
    wide = half.astype(F32)
    weighted = jnp.concatenate(
        [(wide * radial_column(rt_ref, l, field.shape)).astype(BF) for l in range(terms)], axis=1
    )
    per = 1 + len(ROUTED)
    slots = pieces_ref.shape[1:]
    pieces_ref[h * per] = wide.reshape(slots)
    for start in range(0, len(ROUTED), 2):
        pair = ROUTED[start : start + 2]
        rhs = jnp.concatenate([blocks_ref[0, 0, 1 + j].reshape(terms * width, width) for j in pair], axis=1)
        out = dot_nn(weighted, rhs)
        for k in range(len(pair)):
            pieces_ref[h * per + 1 + start + k] = out[:, k * width : (k + 1) * width].reshape(slots)


def emit_pieces(pieces_ref, send_ref):
    count = pieces_ref.shape[0]
    rows, width = pieces_ref.shape[2:]

    def step(i, carry):
        for u in range(2):
            n = 2 * i + u
            send_ref[n] = pieces_ref[:, n].reshape(count * rows, width).astype(BF)
        return carry

    lax.fori_loop(0, send_ref.shape[0] // 2, step, 0)


def emit_edges(h, last, field, cor_ref, up_ref, down_ref):
    @pl.when(h == last)
    def _():
        up_ref[...] = (field * cor_ref[last : last + 1, :]).astype(BF)

    @pl.when(h == 0)
    def _():
        down_ref[...] = field.astype(BF)


def first_kernel(remaining_ref, psi_ref, blocks_ref, rt_ref, cor_ref, field_ref, send_ref, up_ref, down_ref, pieces_ref):
    h = pl.program_id(0)
    last = pl.num_programs(0) - 1
    field = psi_ref[0].T * active_row(remaining_ref, h, psi_ref.shape[1])
    field_ref[0] = field
    emit_edges(h, cor_ref.shape[0] - 1, field, cor_ref, up_ref, down_ref)
    emit_products(h, field, blocks_ref, rt_ref, pieces_ref)

    @pl.when(h == last)
    def _():
        emit_pieces(pieces_ref, send_ref)


def route_kernel(offsets_ref, got_ref, send_ref, wide_ref):
    count, rows, width = got_ref.shape
    helicities = offsets_ref.shape[0]
    per = 1 + len(ROUTED)
    piece = rows // (helicities * per)

    def widen(b, carry):
        for u in range(2):
            wide_ref[2 * b + u] = got_ref[2 * b + u].astype(F32)
        return carry

    lax.fori_loop(0, count // 2, widen, 0)

    def step(d, carry):
        out = []
        for h in range(helicities):
            base = h * per * piece
            total = None
            for k, j in enumerate(ROUTED):
                turn = offsets_ref[h, j]
                ahead = (d + turn) & (count - 1)
                behind = (d - turn) & (count - 1)
                out.append(wide_ref[ahead, base : base + piece, :])
                at = base + (1 + k) * piece
                term = wide_ref[behind, at : at + piece, :]
                total = term if total is None else total + term
            out.append(total)
        send_ref[d] = jnp.concatenate(out, axis=0).astype(BF)
        return carry

    lax.fori_loop(0, count, step, 0)


def local_kernel(
    transposed, remaining_ref, field_ref, prev_ref, diag_ref, rt_ref, kin_ref, cent_ref, damp_ref, e_ref, rot_ref, cor_ref, out_ref
):
    helicities, points, width = field_ref.shape
    terms = diag_ref.shape[3 - 1]
    cent = cent_ref[...]
    damp = damp_ref[...]
    for h in range(helicities):
        mask = active_row(remaining_ref, h, width)
        field = field_ref[h]
        half = field.astype(BF)
        total = lax.dot_general(
            kin_ref[...], field, (((1,), (0,)), ((), ())), precision=lax.Precision.HIGHEST, preferred_element_type=F32
        )
        for l in range(terms):
            block = diag_ref[h, 0, l]
            total = total + radial_column(rt_ref, l, field.shape) * (dot_nn(half, block) + dot_nt(half, block))
        total = total + (e_ref[h : h + 1, :] + cent * rot_ref[h : h + 1, :]) * field
        if h + 1 < helicities:
            total = total - cent * (cor_ref[h : h + 1, :] * field_ref[h + 1])
        if h > 0:
            total = total - cent * (cor_ref[h - 1 : h, :] * field_ref[h - 1])
        previous = prev_ref[h] if transposed else prev_ref[h].T * mask
        out_ref[h] = damp * (2.0 * (mask * total) - damp * previous)


def renew(h, remaining_ref, local_ref, sources_ref, blocks_ref, rt_ref, cent_ref, damp_ref, cor_ref, below_ref, above_ref):
    _, points, width = local_ref.shape
    terms = blocks_ref.shape[3]
    helicities = cor_ref.shape[0]
    per = 1 + len(ROUTED)
    shape = (points, width)
    sources = jnp.concatenate(
        [sources_ref[h * per + k].reshape(shape).astype(BF) for k in range(len(ROUTED))], axis=1
    )
    total = sources_ref[h * per + len(ROUTED)].reshape(shape)
    for l in range(0, terms, 2):
        rhs = jnp.concatenate(
            [jnp.concatenate([blocks_ref[0, 0, 1 + j, l + u] for j in ROUTED], axis=1) for u in range(2)], axis=0
        )
        out = dot_nt(sources, rhs)
        for u in range(2):
            total = total + radial_column(rt_ref, l + u, shape) * out[:, u * width : (u + 1) * width]
    below = jnp.where(h == 0, 1.0, 0.0) * below_ref[...].astype(F32)
    above = jnp.where(h == helicities - 1, 1.0, 0.0) * above_ref[...].astype(F32) * cor_ref[helicities - 1 : helicities, :]
    total = total - cent_ref[...] * (below + above)
    return local_ref[0] + 2.0 * damp_ref[...] * (active_row(remaining_ref, h, width) * total)


def unpack(got_ref, sources_ref):
    count, rows, width = got_ref.shape
    slots, _, piece, _ = sources_ref.shape

    def step(i, carry):
        for u in range(2):
            n = 2 * i + u
            sources_ref[:, n] = got_ref[n].astype(F32).reshape(slots, piece, width)
        return carry

    lax.fori_loop(0, count // 2, step, 0)


def middle_kernel(
    remaining_ref, got_ref, local_ref, blocks_ref, rt_ref, cent_ref, damp_ref, cor_ref, below_ref, above_ref,
    field_ref, send_ref, up_ref, down_ref, sources_ref, pieces_ref,
):
    h = pl.program_id(0)

    @pl.when(h == 0)
    def _():
        unpack(got_ref, sources_ref)

    field = renew(
        h, remaining_ref, local_ref, sources_ref, blocks_ref, rt_ref, cent_ref, damp_ref, cor_ref, below_ref, above_ref
    )
    field_ref[0] = field
    emit_edges(h, cor_ref.shape[0] - 1, field, cor_ref, up_ref, down_ref)
    emit_products(h, field, blocks_ref, rt_ref, pieces_ref)

    @pl.when(h == pl.num_programs(0) - 1)
    def _():
        emit_pieces(pieces_ref, send_ref)


def last_kernel(
    remaining_ref, got_ref, local_ref, blocks_ref, rt_ref, cent_ref, damp_ref, cor_ref, below_ref, above_ref, field_ref,
    before_ref, last_ref, sources_ref,
):
    h = pl.program_id(0)

    @pl.when(h == 0)
    def _():
        unpack(got_ref, sources_ref)

    field = renew(
        h, remaining_ref, local_ref, sources_ref, blocks_ref, rt_ref, cent_ref, damp_ref, cor_ref, below_ref, above_ref
    )
    last_ref[0] = field.T
    before_ref[0] = field_ref[0].T


def shifted(x, axis, by):
    peers = lax.axis_size(axis)
    return lax.ppermute(x, axis, [(i, i + by) for i in range(peers) if 0 <= i + by < peers])


def exchange(x):
    return lax.all_to_all(x, "chan", 0, 0, tiled=True)


def body(psi_prev, psi_cur, blocks, radial_terms, energies, rotation, coriolis, counts, offsets):
    helicities, width, points = psi_cur.shape
    count = lax.axis_size("chan")
    terms = blocks.shape[3]
    piece = points // count
    per = 1 + len(ROUTED)
    rows = helicities * per * piece
    remaining = counts - lax.axis_index("chan").astype(jnp.int32) * width
    rt = radial_terms.T
    kinetic = jnp.asarray(kinetic_matrix(points))
    cent, damp = (jnp.asarray(v) for v in radial_profiles(points, width))

    smem = pl.BlockSpec(memory_space=pltpu.SMEM)
    whole = lambda a: pl.BlockSpec(a, lambda *_: (0,) * len(a))
    by_h = lambda a: pl.BlockSpec((1,) + a[1:], lambda h: (h,) + (0,) * (len(a) - 1))
    sds = jax.ShapeDtypeStruct
    params = lambda: pltpu.CompilerParams(vmem_limit_bytes=VMEM_LIMIT)
    cost = lambda flops, moved: pl.CostEstimate(flops=flops, bytes_accessed=moved, transcendentals=0)

    field_shape = (helicities, points, width)
    field_out = sds(field_shape, F32)
    parcel = sds((count, rows, width), BF)
    edge = sds((points, width), BF)
    parts = pltpu.VMEM((helicities * per, count, piece, width), F32)
    mac = 2 * helicities * points * width * width * terms
    side = blocks.shape[2] - 1

    first = pl.pallas_call(
        first_kernel,
        grid=(helicities,),
        in_specs=[smem, by_h(psi_cur.shape), by_h(blocks.shape), whole(rt.shape), whole(coriolis.shape)],
        out_specs=[by_h(field_shape), whole(parcel.shape), whole(edge.shape), whole(edge.shape)],
        out_shape=[field_out, parcel, edge, edge],
        scratch_shapes=[parts],
        compiler_params=params(),
        cost_estimate=cost(side * mac, blocks.size * 2),
    )
    route = pl.pallas_call(
        route_kernel,
        in_specs=[smem, whole(parcel.shape)],
        out_specs=whole(parcel.shape),
        out_shape=parcel,
        grid=(1,),
        scratch_shapes=[pltpu.VMEM(parcel.shape, F32)],
        compiler_params=params(),
        cost_estimate=cost(parcel.size * 4, parcel.size * 4),
    )

    def local(transposed, prev):
        diag = (helicities, 1, 1) + blocks.shape[3:]

        def kernel(remaining_ref, field_ref, prev_ref, diag_ref, *rest):
            local_kernel(transposed, remaining_ref, field_ref, prev_ref, diag_ref.at[:, 0], *rest)

        return pl.pallas_call(
            kernel,
            grid=(1,),
            in_specs=[
                smem, whole(field_shape), whole(prev.shape), whole(diag), whole(rt.shape), whole(kinetic.shape), whole(cent.shape),
                whole(damp.shape), whole(energies.shape), whole(rotation.shape), whole(coriolis.shape),
            ],
            out_specs=whole(field_shape),
            out_shape=field_out,
            compiler_params=params(),
            cost_estimate=cost(2 * mac, 4 * psi_cur.size),
        )

    renew_specs = [
        smem, whole(parcel.shape), by_h(field_shape), by_h(blocks.shape), whole(rt.shape), whole(cent.shape), whole(damp.shape),
        whole(coriolis.shape), whole(edge.shape), whole(edge.shape),
    ]
    middle = pl.pallas_call(
        middle_kernel,
        grid=(helicities,),
        in_specs=renew_specs,
        out_specs=[by_h(field_shape), whole(parcel.shape), whole(edge.shape), whole(edge.shape)],
        out_shape=[field_out, parcel, edge, edge],
        scratch_shapes=[parts, parts],
        compiler_params=params(),
        cost_estimate=cost(2 * side * mac, blocks.size * 2),
    )
    final = pl.pallas_call(
        last_kernel,
        grid=(helicities,),
        in_specs=renew_specs + [by_h(field_shape)],
        out_specs=[by_h(psi_cur.shape), by_h(psi_cur.shape)],
        out_shape=[sds(psi_cur.shape, F32)] * 2,
        scratch_shapes=[parts],
        compiler_params=params(),
        cost_estimate=cost(side * mac, blocks.size * 2),
    )

    field, send, up, down = first(remaining, psi_cur, blocks, rt, coriolis)
    prev = psi_prev
    for iteration in range(STEPS):
        below = shifted(up, "hel", 1)
        above = shifted(down, "hel", -1)
        got = exchange(send)
        rest = local(iteration > 0, prev)(
            remaining, field, prev, blocks, rt, kinetic, cent, damp, energies, rotation, coriolis
        )
        back = exchange(route(offsets, got))
        given = (remaining, back, rest, blocks, rt, cent, damp, coriolis, below, above)
        prev = field
        if iteration + 1 < STEPS:
            field, send, up, down = middle(*given)
        else:
            return tuple(final(*given, field))


def solution(mesh):
    in_specs = (
        P("hel", "chan", None),
        P("hel", "chan", None),
        P("hel", "chan", None, None, None, None),
        P(),
        P("hel", "chan"),
        P("hel", "chan"),
        P("hel", "chan"),
        P("hel"),
        P("hel", None),
    )
    out_specs = (P("hel", "chan", None), P("hel", "chan", None))
    return jax.shard_map(body, mesh=mesh, in_specs=in_specs, out_specs=out_specs, check_vma=False)
```

```python
import functools

import jax
import jax.numpy as jnp
import numpy as np
from jax import lax
from jax.experimental import pallas as pl
from jax.experimental.pallas import tpu as pltpu
from jax.sharding import PartitionSpec as P

STEPS = 2
BF = jnp.bfloat16
F32 = jnp.float32
VMEM_LIMIT = 24 * 1024 * 1024
SIDES = 7


def kinetic_matrix(points):
    n = points + 1
    i = np.arange(1, n, dtype=np.float64)[:, None]
    k = i.T
    gap = np.where(i == k, 1.0, i - k)
    parity = 1.0 - 2.0 * (np.abs(i - k) % 2)
    off = parity * (1.0 / np.sin(np.pi * gap / (2 * n)) ** 2 - 1.0 / np.sin(np.pi * (i + k) / (2 * n)) ** 2)
    diagonal = (2.0 * n * n + 1.0) / 3.0 - 1.0 / np.sin(np.pi * i / n) ** 2
    return (np.where(i == k, diagonal, off) * (0.25 / (n * n))).astype(np.float32)


def radial_profiles(points, width):
    r = np.arange(points, dtype=np.float64)
    centrifugal = 0.1 / (1.0 + 8.0 * r / points) ** 2
    damping = np.exp(-0.002 * np.maximum(r - 3 * points // 4, 0.0) ** 2)
    spread = lambda v: np.ascontiguousarray(np.broadcast_to(v.astype(np.float32)[:, None], (points, width)))
    return spread(centrifugal), spread(damping)


def dot_nn(a, b):
    return lax.dot_general(a, b, (((1,), (0,)), ((), ())), preferred_element_type=F32)


def dot_nt(a, b):
    return lax.dot_general(a, b, (((1,), (1,)), ((), ())), preferred_element_type=F32)


def active_row(counts_ref, h, width):
    channel = lax.axis_index("chan") * width + lax.broadcasted_iota(jnp.int32, (1, width), 1)
    return (channel < counts_ref[h]).astype(F32)


def radial_columns(radial_ref, shape):
    columns = radial_ref[...].T
    return [jnp.broadcast_to(columns[:, l : l + 1], shape) for l in range(columns.shape[1])]


def weight(wide, columns):
    return jnp.concatenate([(wide * column).astype(BF) for column in columns], axis=1)


def interleave(a, b, count):
    pieces = (count, -1, a.shape[1])
    return jnp.concatenate([a.reshape(pieces), b.reshape(pieces)], axis=1).astype(BF)


def emit_products(field, blocks_ref, columns, send_ref, arrived=None):
    width = field.shape[1]
    count, rows = send_ref.shape[:2]
    pair = rows // 4
    wide = field.astype(BF).astype(F32)
    weighted = jnp.concatenate([(wide * column).astype(BF) for column in columns], axis=1)
    if arrived is not None:
        arrived()
    send_ref[:, :pair, :] = interleave(wide, dot_nn(weighted, blocks_ref[0].reshape(-1, width)), count)
    for p in range(1, 4):
        rhs = [blocks_ref[j].reshape(-1, width) for j in (2 * p - 1, 2 * p)]
        out = dot_nn(weighted, jnp.concatenate(rhs, axis=1))
        send_ref[:, p * pair : (p + 1) * pair, :] = interleave(out[:, :width], out[:, width:], count)


def fetch(blocks_ref, kept_ref, sem):
    copies = []
    for h in range(blocks_ref.shape[0]):
        copies.append([])
        for k, at in enumerate(range(0, SIDES, 2)):
            size = min(2, SIDES - at)
            source = blocks_ref.at[h, 0, pl.ds(1 + at, size)]
            copies[h].append(pltpu.make_async_copy(source, kept_ref.at[h, pl.ds(at, size)], sem.at[h, k]))
            copies[h][-1].start()

    def arrive(h):
        for copy in copies[h]:
            copy.wait()

    return [functools.partial(arrive, h) for h in range(len(copies))]


def emit_edges(h, field, cor_ref, up_ref, down_ref):
    last = cor_ref.shape[0] - 1
    if h == last:
        up_ref[...] = (field * cor_ref[last : last + 1, :]).astype(BF)
    if h == 0:
        down_ref[...] = field.astype(BF)


def copy_out(h, made_ref, send_ref, sem):
    rows = made_ref.shape[2]
    copy = pltpu.make_async_copy(made_ref.at[h], send_ref.at[:, pl.ds(h * rows, rows), :], sem.at[h])
    copy.start()
    return copy


def first_kernel(
    counts_ref, radial_ref, cor_ref, psi_ref, blocks_ref, field_ref, up_ref, down_ref, send_ref,
    here_ref, kept_ref, made_ref, psi_sem, block_sem, send_sem,
):
    helicities, _, width = field_ref.shape
    psi = [pltpu.make_async_copy(psi_ref.at[h], here_ref.at[h], psi_sem.at[h]) for h in range(helicities)]
    psi[0].start()
    arrived = fetch(blocks_ref, kept_ref, block_sem)
    for copy in psi[1:]:
        copy.start()
    columns = radial_columns(radial_ref, field_ref.shape[1:])
    sent = []
    for h in range(helicities):
        psi[h].wait()
        field = here_ref[h].T * active_row(counts_ref, h, width)
        field_ref[h] = field
        emit_edges(h, field, cor_ref, up_ref, down_ref)
        emit_products(field, kept_ref.at[h], columns, made_ref.at[h], arrived[h])
        sent.append(copy_out(h, made_ref, send_ref, send_sem))
    for copy in sent:
        copy.wait()


def route_kernel(offsets_ref, got_ref, *refs):
    send_ref, wide_ref = refs[-2:]
    count = got_ref.shape[0]
    helicities = offsets_ref.shape[0]
    rows = got_ref.shape[1] // helicities
    piece = rows // (1 + SIDES)
    for h in range(helicities):
        mine = slice(h * rows, (h + 1) * rows)

        def widen(i, carry):
            for u in range(4):
                wide = got_ref[4 * i + u, mine, :].astype(F32)
                wide_ref[4 * i + u] = wide
                wide_ref[4 * i + u + count] = wide
            return carry

        lax.fori_loop(0, count // 4, widen, 0)
        ahead = [wide_ref.at[pl.ds(offsets_ref[h, j], count)] for j in range(SIDES)]
        behind = [wide_ref.at[pl.ds(count - offsets_ref[h, j], count)] for j in range(SIDES)]
        for d in range(count):
            out = [ref[d, :piece, :] for ref in ahead]
            terms = [ref[d, (1 + j) * piece : (2 + j) * piece, :] for j, ref in enumerate(behind)]
            while len(terms) > 1:
                terms = [sum(terms[k + 1 : k + 2], terms[k]) for k in range(0, len(terms), 2)]
            send_ref[d, mine, :] = jnp.concatenate(out + terms, axis=0).astype(BF)


def forward(sources, blocks, columns, total, arrived=None):
    points, width = total.shape
    terms = blocks[0].shape[0]
    sources = jnp.concatenate(sources, axis=1)
    if arrived is not None:
        arrived()
    for l in range(0, terms, 2):
        rhs = jnp.concatenate([jnp.concatenate([b[l + u] for b in blocks], axis=1) for u in range(2)], axis=0)
        out = dot_nt(sources, rhs)
        for u in range(2):
            total = total + columns[l + u] * out[:, u * width : (u + 1) * width]
    return total


def local_kernel(
    final, counts_ref, prev_ref, radial_ref, kin_ref, cent_ref, damp_ref, e_ref, rot_ref, cor_ref, field_ref, blocks_ref, out_ref, *refs
):
    helicities, points, width = field_ref.shape
    terms = blocks_ref.shape[3]
    cent = cent_ref[...]
    damp = damp_ref[...]
    columns = radial_columns(radial_ref, (points, width))
    for h in range(helicities):
        mask = active_row(counts_ref, h, width)
        field = field_ref[h]
        half = field.astype(BF)
        total = lax.dot_general(
            kin_ref[...], field, (((1,), (0,)), ((), ())), precision=lax.Precision.HIGHEST, preferred_element_type=F32
        )
        for l in range(terms):
            total = total + columns[l] * dot_nn(half, blocks_ref[h, 0, 0, l])
        total = forward([half], [blocks_ref.at[h, 0, 0]], columns, total)
        total = total + (e_ref[h : h + 1, :] + cent * rot_ref[h : h + 1, :]) * field
        if h + 1 < helicities:
            total = total - cent * (cor_ref[h : h + 1, :] * field_ref[h + 1])
        if h > 0:
            total = total - cent * (cor_ref[h - 1 : h, :] * field_ref[h - 1])
        previous = prev_ref[h] if final else prev_ref[h].T * mask
        out_ref[h] = damp * (2.0 * (mask * total) - damp * previous)
        if final:
            refs[0][h] = field.T


def renew(h, got_ref, counts_ref, local_ref, columns, cent_ref, damp_ref, cor_ref, below_ref, above_ref, kept_ref, arrived):
    helicities, points, width = local_ref.shape
    rows = got_ref.shape[1] // helicities
    pair = rows // 4
    slots = []
    for p in range(4):
        both = got_ref[:, h * rows + p * pair : h * rows + (p + 1) * pair, :].astype(F32)
        slots += [both[:, : pair // 2].reshape(points, width), both[:, pair // 2 :].reshape(points, width)]
    total = slots[-1]
    if h == 0:
        total = total - cent_ref[...] * below_ref[...].astype(F32)
    if h == helicities - 1:
        total = total - cent_ref[...] * (above_ref[...].astype(F32) * cor_ref[h : h + 1, :])
    sources = [slot.astype(BF) for slot in slots[:-1]]
    total = forward(sources, [kept_ref.at[h, j] for j in range(SIDES)], columns, total, arrived[h])
    return local_ref[h] + 2.0 * damp_ref[...] * (active_row(counts_ref, h, width) * total)


def middle_kernel(
    counts_ref, radial_ref, cent_ref, damp_ref, cor_ref, got_ref, local_ref, below_ref, above_ref, blocks_ref,
    field_ref, up_ref, down_ref, send_ref, kept_ref, made_ref, block_sem, send_sem,
):
    arrived = fetch(blocks_ref, kept_ref, block_sem)
    columns = radial_columns(radial_ref, local_ref.shape[1:])
    sent = []
    for h in range(local_ref.shape[0]):
        field = renew(
            h, got_ref, counts_ref, local_ref, columns, cent_ref, damp_ref, cor_ref, below_ref, above_ref, kept_ref, arrived
        )
        field_ref[h] = field
        emit_edges(h, field, cor_ref, up_ref, down_ref)
        emit_products(field, kept_ref.at[h], columns, made_ref.at[h])
        sent.append(copy_out(h, made_ref, send_ref, send_sem))
    for copy in sent:
        copy.wait()


def last_kernel(
    counts_ref, radial_ref, cent_ref, damp_ref, cor_ref, got_ref, local_ref, below_ref, above_ref, blocks_ref, out_ref,
    kept_ref, made_ref, block_sem, sem,
):
    arrived = fetch(blocks_ref, kept_ref, block_sem)
    columns = radial_columns(radial_ref, local_ref.shape[1:])
    sent = []
    for h in range(local_ref.shape[0]):
        field = renew(
            h, got_ref, counts_ref, local_ref, columns, cent_ref, damp_ref, cor_ref, below_ref, above_ref, kept_ref, arrived
        )
        made_ref[h] = field.T
        copy = pltpu.make_async_copy(made_ref.at[h], out_ref.at[h], sem.at[h])
        copy.start()
        sent.append(copy)
    for copy in sent:
        copy.wait()


def shifted(x, axis, by):
    peers = lax.axis_size(axis)
    return lax.ppermute(x, axis, [(i, i + by) for i in range(peers) if 0 <= i + by < peers])


def exchange(x):
    return lax.all_to_all(x, "chan", 0, 0, tiled=True)


def body(psi_prev, psi_cur, blocks, radial_terms, energies, rotation, coriolis, counts, offsets):
    helicities, width, points = psi_cur.shape
    count = lax.axis_size("chan")
    terms = blocks.shape[3]
    rows = (1 + SIDES) * points // count
    assert blocks.shape[2] == offsets.shape[1] + 1 == SIDES + 1
    kinetic = jnp.asarray(kinetic_matrix(points))
    cent, damp = (jnp.asarray(v) for v in radial_profiles(points, width))

    smem = pl.BlockSpec(memory_space=pltpu.SMEM)
    vmem = pl.BlockSpec(memory_space=pltpu.VMEM)
    hbm = pl.BlockSpec(memory_space=pl.ANY)
    whole = lambda a: pl.BlockSpec(a.shape, lambda *_: (0,) * a.ndim)
    place = lambda a: pltpu.with_memory_space_constraint(a, pltpu.HBM)
    psi_cur, psi_prev, blocks, radial_terms, counts, offsets = map(
        place, (psi_cur, psi_prev, blocks, radial_terms, counts, offsets)
    )

    field_shape = (helicities, points, width)
    field_out = pltpu.VMEM(field_shape, F32)
    parcel_shape = (count, helicities * rows, width)
    parcel_out = pltpu.HBM(parcel_shape, BF)
    edge_out = pltpu.HBM((points, width), BF)
    edge = pl.BlockSpec(edge_out.shape, lambda *_: (0, 0))
    made = pltpu.VMEM((helicities, count, rows, width), BF)
    kept = pltpu.VMEM((helicities, SIDES) + blocks.shape[3:], BF)
    copies = pltpu.SemaphoreType.DMA((helicities,))
    parts = pltpu.SemaphoreType.DMA((helicities, (SIDES + 1) // 2))
    diagonal = pl.BlockSpec((helicities, 1, 1) + blocks.shape[3:], lambda *_: (0,) * blocks.ndim)
    mac = 2 * helicities * points * width * width * terms

    def call(kernel, in_specs, out_specs, out_shape, flops, moved, scratch=()):
        return pl.pallas_call(
            kernel,
            grid=(1,),
            in_specs=in_specs,
            out_specs=out_specs,
            out_shape=out_shape,
            scratch_shapes=scratch,
            compiler_params=pltpu.CompilerParams(vmem_limit_bytes=VMEM_LIMIT),
            cost_estimate=pl.CostEstimate(flops=flops, bytes_accessed=moved, transcendentals=0),
        )

    first = call(
        first_kernel,
        [smem, whole(radial_terms), whole(coriolis), hbm, hbm],
        [vmem, edge, edge, hbm],
        [field_out, edge_out, edge_out, parcel_out],
        SIDES * mac,
        blocks.size * 2,
        [pltpu.VMEM(psi_cur.shape, F32), kept, made, copies, parts, copies],
    )
    route = call(
        route_kernel,
        [smem, vmem, hbm, hbm, hbm],
        vmem,
        pltpu.VMEM(parcel_shape, BF),
        psi_cur.size * 8,
        psi_cur.size * 4,
        [pltpu.VMEM((2 * count, rows, width), F32)],
    )

    def local(final):
        kernel = functools.partial(local_kernel, final)
        tables = [whole(a) for a in (psi_prev, radial_terms, kinetic, cent, damp, energies, rotation, coriolis)]
        if final:
            tables[0] = vmem
        out_specs = [vmem, whole(psi_prev)] if final else vmem
        out_shape = [field_out, pltpu.HBM(psi_prev.shape, F32)] if final else field_out
        return call(kernel, [smem] + tables + [vmem, diagonal], out_specs, out_shape, 2 * mac, 4 * psi_cur.size)

    given = [smem, *[whole(a) for a in (radial_terms, cent, damp, coriolis)], vmem, vmem, edge, edge, hbm]
    middle = call(
        middle_kernel,
        given,
        [vmem, edge, edge, hbm],
        [field_out, edge_out, edge_out, parcel_out],
        2 * SIDES * mac,
        blocks.size,
        [kept, made, parts, copies],
    )
    final = call(
        last_kernel,
        given,
        hbm,
        pltpu.HBM(psi_cur.shape, F32),
        SIDES * mac,
        blocks.size,
        [kept, pltpu.VMEM(psi_cur.shape, F32), parts, copies],
    )

    field, up, down, send = first(counts, radial_terms, coriolis, psi_cur, blocks)
    prev = psi_prev
    for iteration in range(STEPS):
        ends = iteration + 1 == STEPS
        got = exchange(send)
        below = shifted(up, "hel", 1)
        above = shifted(down, "hel", -1)
        rest = local(iteration > 0)(
            counts, prev, radial_terms, kinetic, cent, damp, energies, rotation, coriolis, field, blocks
        )
        if ends:
            rest, before = rest
        back = exchange(route(offsets, got, rest, below, above))
        given = (counts, radial_terms, cent, damp, coriolis, back, rest, below, above, blocks)
        if ends:
            return before, final(*given)
        prev = field
        field, up, down, send = middle(*given)


def solution(mesh):
    in_specs = (
        P("hel", "chan", None),
        P("hel", "chan", None),
        P("hel", "chan", None, None, None, None),
        P(),
        P("hel", "chan"),
        P("hel", "chan"),
        P("hel", "chan"),
        P("hel"),
        P("hel", None),
    )
    out_specs = (P("hel", "chan", None), P("hel", "chan", None))
    return jax.shard_map(body, mesh=mesh, in_specs=in_specs, out_specs=out_specs, check_vma=False)
```

```python
import functools

import jax
import jax.numpy as jnp
import numpy as np
from jax import lax
from jax.experimental import pallas as pl
from jax.experimental.pallas import tpu as pltpu
from jax.sharding import PartitionSpec as P

STEPS = 2
BF = jnp.bfloat16
F32 = jnp.float32
VMEM_LIMIT = 24 * 1024 * 1024
SIDES = 7


def kinetic_matrix(points):
    n = points + 1
    i = np.arange(1, n, dtype=np.float64)[:, None]
    k = i.T
    gap = np.where(i == k, 1.0, i - k)
    parity = 1.0 - 2.0 * (np.abs(i - k) % 2)
    off = parity * (1.0 / np.sin(np.pi * gap / (2 * n)) ** 2 - 1.0 / np.sin(np.pi * (i + k) / (2 * n)) ** 2)
    diagonal = (2.0 * n * n + 1.0) / 3.0 - 1.0 / np.sin(np.pi * i / n) ** 2
    return (np.where(i == k, diagonal, off) * (0.25 / (n * n))).astype(np.float32)


def radial_profiles(points, width):
    r = np.arange(points, dtype=np.float64)
    centrifugal = 0.1 / (1.0 + 8.0 * r / points) ** 2
    damping = np.exp(-0.002 * np.maximum(r - 3 * points // 4, 0.0) ** 2)
    spread = lambda v: np.ascontiguousarray(np.broadcast_to(v.astype(np.float32)[:, None], (points, width)))
    return spread(centrifugal), spread(damping)


def dot_nn(a, b):
    return lax.dot_general(a, b, (((1,), (0,)), ((), ())), preferred_element_type=F32)


def dot_nt(a, b):
    return lax.dot_general(a, b, (((1,), (1,)), ((), ())), preferred_element_type=F32)


def active_row(counts_ref, h, width):
    channel = lax.axis_index("chan") * width + lax.broadcasted_iota(jnp.int32, (1, width), 1)
    return (channel < counts_ref[h]).astype(F32)


def radial_columns(radial_ref, columns_ref):
    columns = radial_ref[...].T
    for l in range(columns.shape[1]):
        columns_ref[l] = jnp.broadcast_to(columns[:, l : l + 1], columns_ref.shape[1:])


def weight(wide, columns):
    return jnp.concatenate([(wide * columns[l]).astype(BF) for l in range(columns.shape[0])], axis=1)


def interleave(a, b, count):
    pieces = (count, -1, a.shape[1])
    return jnp.concatenate([a.reshape(pieces), b.reshape(pieces)], axis=1).astype(BF)


def emit_products(field, blocks_ref, columns, send_ref, arrived=None):
    width = field.shape[1]
    count, rows = send_ref.shape[:2]
    pair = rows // 4
    wide = field.astype(BF).astype(F32)
    weighted = jnp.concatenate([(wide * columns[l]).astype(BF) for l in range(columns.shape[0])], axis=1)
    if arrived is not None:
        arrived()
    send_ref[:, :pair, :] = interleave(wide, dot_nn(weighted, blocks_ref[0].reshape(-1, width)), count)
    for p in range(1, 4):
        rhs = [blocks_ref[j].reshape(-1, width) for j in (2 * p - 1, 2 * p)]
        out = dot_nn(weighted, jnp.concatenate(rhs, axis=1))
        send_ref[:, p * pair : (p + 1) * pair, :] = interleave(out[:, :width], out[:, width:], count)


def fetch(blocks_ref, kept_ref, sem):
    copies = []
    for h in range(blocks_ref.shape[0]):
        copies.append([])
        for k, at in enumerate(range(0, SIDES, 2)):
            size = min(2, SIDES - at)
            source = blocks_ref.at[h, 0, pl.ds(1 + at, size)]
            copies[h].append(pltpu.make_async_copy(source, kept_ref.at[h, pl.ds(at, size)], sem.at[h, k]))
            copies[h][-1].start()

    def arrive(h):
        for copy in copies[h]:
            copy.wait()

    return [functools.partial(arrive, h) for h in range(len(copies))]


def odd_group():
    return lax.rem(lax.axis_index("hel"), 2) == 1


def emit_edges(fields_ref, cor_ref, edge_ref, inner_ref, outer_ref, sem):
    last = cor_ref.shape[0] - 1
    up = (fields_ref[last] * cor_ref[last : last + 1, :]).astype(BF)
    down = fields_ref[0].astype(BF)
    edge_ref[0] = jnp.where(odd_group(), down, up)
    edge_ref[1] = jnp.where(odd_group(), up, down)
    copies = [pltpu.make_async_copy(edge_ref.at[k], ref, sem.at[k]) for k, ref in enumerate((inner_ref, outer_ref))]
    for copy in copies:
        copy.start()
    return copies


def copy_out(h, made_ref, send_ref, sem):
    rows = made_ref.shape[2]
    copy = pltpu.make_async_copy(made_ref.at[h], send_ref.at[:, pl.ds(h * rows, rows), :], sem.at[h])
    copy.start()
    return copy


def first_kernel(
    counts_ref, radial_hbm, cor_hbm, psi_ref, blocks_ref, field_ref, inner_ref, outer_ref, send_ref,
    here_ref, radial_ref, cor_ref, columns_ref, kept_ref, made_ref, edge_ref, small_sem, psi_sem, block_sem, edge_sem, send_sem,
):
    helicities, _, width = field_ref.shape
    psi = [pltpu.make_async_copy(psi_ref.at[h], here_ref.at[h], psi_sem.at[h]) for h in range(helicities)]
    small = [
        pltpu.make_async_copy(radial_hbm, radial_ref, small_sem.at[0]),
        pltpu.make_async_copy(cor_hbm, cor_ref, small_sem.at[1]),
    ]
    for copy in small + psi:
        copy.start()
    arrived = fetch(blocks_ref, kept_ref, block_sem)
    for copy in small:
        copy.wait()
    radial_columns(radial_ref, columns_ref)
    sent = []
    for h in range(helicities):
        psi[h].wait()
        field = here_ref[h].T * active_row(counts_ref, h, width)
        field_ref[h] = field
        emit_products(field, kept_ref.at[h], columns_ref, made_ref.at[h], arrived[h])
        sent.append(copy_out(h, made_ref, send_ref, send_sem))
    sent += emit_edges(field_ref, cor_ref, edge_ref, inner_ref, outer_ref, edge_sem)
    for copy in sent:
        copy.wait()


def route_kernel(offsets_ref, got_ref, *refs):
    send_ref, wide_ref = refs[-2:]
    count = got_ref.shape[0]
    helicities = offsets_ref.shape[0]
    rows = got_ref.shape[1] // helicities
    piece = rows // (1 + SIDES)
    for h in range(helicities):
        mine = slice(h * rows, (h + 1) * rows)

        def widen(i, carry):
            for u in range(4):
                wide = got_ref[4 * i + u, mine, :].astype(F32)
                wide_ref[4 * i + u] = wide
                wide_ref[4 * i + u + count] = wide
            return carry

        lax.fori_loop(0, count // 4, widen, 0)
        ahead = [wide_ref.at[pl.ds(offsets_ref[h, j], count)] for j in range(SIDES)]
        behind = [wide_ref.at[pl.ds(count - offsets_ref[h, j], count)] for j in range(SIDES)]
        for d in range(count):
            out = [ref[d, :piece, :] for ref in ahead]
            terms = [ref[d, (1 + j) * piece : (2 + j) * piece, :] for j, ref in enumerate(behind)]
            while len(terms) > 1:
                terms = [sum(terms[k + 1 : k + 2], terms[k]) for k in range(0, len(terms), 2)]
            send_ref[d, mine, :] = jnp.concatenate(out + terms, axis=0).astype(BF)


def forward(sources, blocks, columns, total, arrived=None):
    points, width = total.shape
    terms = blocks[0].shape[0]
    sources = jnp.concatenate(sources, axis=1)
    if arrived is not None:
        arrived()
    for l in range(0, terms, 2):
        rhs = jnp.concatenate([jnp.concatenate([b[l + u] for b in blocks], axis=1) for u in range(2)], axis=0)
        out = dot_nt(sources, rhs)
        for u in range(2):
            total = total + columns[l + u] * out[:, u * width : (u + 1) * width]
    return total


def local_kernel(
    final, counts_ref, prev_ref, radial_ref, kin_ref, cent_ref, damp_ref, e_ref, rot_ref, cor_ref, field_ref, blocks_ref, out_ref, *refs
):
    helicities, points, width = field_ref.shape
    terms = blocks_ref.shape[3]
    cent = cent_ref[...]
    damp = damp_ref[...]
    columns = refs[-1]
    radial_columns(radial_ref, columns)
    for h in range(helicities):
        mask = active_row(counts_ref, h, width)
        field = field_ref[h]
        half = field.astype(BF)
        total = lax.dot_general(
            kin_ref[...], field, (((1,), (0,)), ((), ())), precision=lax.Precision.HIGHEST, preferred_element_type=F32
        )
        for l in range(terms):
            total = total + columns[l] * dot_nn(half, blocks_ref[h, 0, 0, l])
        total = forward([half], [blocks_ref.at[h, 0, 0]], columns, total)
        total = total + (e_ref[h : h + 1, :] + cent * rot_ref[h : h + 1, :]) * field
        if h + 1 < helicities:
            total = total - cent * (cor_ref[h : h + 1, :] * field_ref[h + 1])
        if h > 0:
            total = total - cent * (cor_ref[h - 1 : h, :] * field_ref[h - 1])
        previous = prev_ref[h] if final else prev_ref[h].T * mask
        out_ref[h] = damp * (2.0 * (mask * total) - damp * previous)
        if final:
            refs[0][h] = field.T


def renew(h, got_ref, counts_ref, local_ref, columns, cent_ref, damp_ref, cor_ref, inner_ref, outer_ref, kept_ref, arrived):
    helicities, points, width = local_ref.shape
    rows = got_ref.shape[1] // helicities
    pair = rows // 4
    slots = []
    for p in range(4):
        both = got_ref[:, h * rows + p * pair : h * rows + (p + 1) * pair, :].astype(F32)
        slots += [both[:, : pair // 2].reshape(points, width), both[:, pair // 2 :].reshape(points, width)]
    total = slots[-1]
    if h == 0:
        below = jnp.where(odd_group(), inner_ref[...], outer_ref[...])
        total = total - cent_ref[...] * below.astype(F32)
    if h == helicities - 1:
        above = jnp.where(odd_group(), outer_ref[...], inner_ref[...])
        total = total - cent_ref[...] * (above.astype(F32) * cor_ref[h : h + 1, :])
    sources = [slot.astype(BF) for slot in slots[:-1]]
    total = forward(sources, [kept_ref.at[h, j] for j in range(SIDES)], columns, total, arrived[h])
    return local_ref[h] + 2.0 * damp_ref[...] * (active_row(counts_ref, h, width) * total)


def middle_kernel(
    counts_ref, radial_ref, cent_ref, damp_ref, cor_ref, got_ref, local_ref, inner_got, outer_got, blocks_ref,
    field_ref, inner_ref, outer_ref, send_ref, columns, kept_ref, made_ref, edge_ref, block_sem, edge_sem, send_sem,
):
    arrived = fetch(blocks_ref, kept_ref, block_sem)
    radial_columns(radial_ref, columns)
    sent = []
    for h in range(local_ref.shape[0]):
        field = renew(
            h, got_ref, counts_ref, local_ref, columns, cent_ref, damp_ref, cor_ref, inner_got, outer_got, kept_ref, arrived
        )
        field_ref[h] = field
        emit_products(field, kept_ref.at[h], columns, made_ref.at[h])
        sent.append(copy_out(h, made_ref, send_ref, send_sem))
    sent += emit_edges(field_ref, cor_ref, edge_ref, inner_ref, outer_ref, edge_sem)
    for copy in sent:
        copy.wait()


def last_kernel(
    counts_ref, radial_ref, cent_ref, damp_ref, cor_ref, got_ref, local_ref, inner_got, outer_got, blocks_ref, out_ref,
    columns, kept_ref, made_ref, block_sem, sem,
):
    arrived = fetch(blocks_ref, kept_ref, block_sem)
    radial_columns(radial_ref, columns)
    sent = []
    for h in range(local_ref.shape[0]):
        field = renew(
            h, got_ref, counts_ref, local_ref, columns, cent_ref, damp_ref, cor_ref, inner_got, outer_got, kept_ref, arrived
        )
        made_ref[h] = field.T
        copy = pltpu.make_async_copy(made_ref.at[h], out_ref.at[h], sem.at[h])
        copy.start()
        sent.append(copy)
    for copy in sent:
        copy.wait()


def swapped(x, axis, first):
    peers = lax.axis_size(axis)
    pairs = [(i, i + 1) for i in range(first, peers - 1, 2)]
    return lax.ppermute(x, axis, pairs + [(j, i) for i, j in pairs])


def exchange(x):
    return lax.all_to_all(x, "chan", 0, 0, tiled=True)


def body(psi_prev, psi_cur, blocks, radial_terms, energies, rotation, coriolis, counts, offsets):
    helicities, width, points = psi_cur.shape
    count = lax.axis_size("chan")
    terms = blocks.shape[3]
    rows = (1 + SIDES) * points // count
    assert blocks.shape[2] == offsets.shape[1] + 1 == SIDES + 1
    kinetic = jnp.asarray(kinetic_matrix(points))
    cent, damp = (jnp.asarray(v) for v in radial_profiles(points, width))

    smem = pl.BlockSpec(memory_space=pltpu.SMEM)
    vmem = pl.BlockSpec(memory_space=pltpu.VMEM)
    hbm = pl.BlockSpec(memory_space=pl.ANY)
    whole = lambda a: pl.BlockSpec(a.shape, lambda *_: (0,) * a.ndim)
    place = lambda a: pltpu.with_memory_space_constraint(a, pltpu.HBM)
    psi_cur, psi_prev, blocks, counts, offsets = map(place, (psi_cur, psi_prev, blocks, counts, offsets))

    field_shape = (helicities, points, width)
    field_out = pltpu.VMEM(field_shape, F32)
    parcel_shape = (count, helicities * rows, width)
    parcel_out = pltpu.HBM(parcel_shape, BF)
    edge_out = pltpu.HBM((points, width), BF)
    edges = pltpu.VMEM((2, points, width), BF)
    pair = pltpu.SemaphoreType.DMA((2,))
    columns = pltpu.VMEM((terms, points, width), F32)
    made = pltpu.VMEM((helicities, count, rows, width), BF)
    kept = pltpu.VMEM((helicities, SIDES) + blocks.shape[3:], BF)
    copies = pltpu.SemaphoreType.DMA((helicities,))
    parts = pltpu.SemaphoreType.DMA((helicities, (SIDES + 1) // 2))
    diagonal = pl.BlockSpec((helicities, 1, 1) + blocks.shape[3:], lambda *_: (0,) * blocks.ndim)
    mac = 2 * helicities * points * width * width * terms

    def call(kernel, in_specs, out_specs, out_shape, flops, moved, scratch=()):
        return pl.pallas_call(
            kernel,
            grid=(1,),
            in_specs=in_specs,
            out_specs=out_specs,
            out_shape=out_shape,
            scratch_shapes=scratch,
            compiler_params=pltpu.CompilerParams(vmem_limit_bytes=VMEM_LIMIT),
            cost_estimate=pl.CostEstimate(flops=flops, bytes_accessed=moved, transcendentals=0),
        )

    first = call(
        first_kernel,
        [smem, hbm, hbm, hbm, hbm],
        [vmem, hbm, hbm, hbm],
        [field_out, edge_out, edge_out, parcel_out],
        SIDES * mac,
        blocks.size * 2,
        [
            pltpu.VMEM(psi_cur.shape, F32), pltpu.VMEM(radial_terms.shape, F32), pltpu.VMEM(coriolis.shape, F32), columns, kept,
            made, edges, pair, copies, parts, pair, copies,
        ],
    )
    route = call(
        route_kernel,
        [smem, vmem, hbm, hbm, hbm],
        vmem,
        pltpu.VMEM(parcel_shape, BF),
        psi_cur.size * 8,
        psi_cur.size * 4,
        [pltpu.VMEM((2 * count, rows, width), F32)],
    )

    def local(final):
        kernel = functools.partial(local_kernel, final)
        tables = [whole(a) for a in (psi_prev, radial_terms, kinetic, cent, damp, energies, rotation, coriolis)]
        if final:
            tables[0] = vmem
        out_specs = [vmem, whole(psi_prev)] if final else vmem
        out_shape = [field_out, pltpu.HBM(psi_prev.shape, F32)] if final else field_out
        return call(kernel, [smem] + tables + [vmem, diagonal], out_specs, out_shape, 2 * mac, 4 * psi_cur.size, [columns])

    given = [smem] + [vmem] * 8 + [hbm]
    middle = call(
        middle_kernel,
        given,
        [vmem, hbm, hbm, hbm],
        [field_out, edge_out, edge_out, parcel_out],
        2 * SIDES * mac,
        blocks.size,
        [columns, kept, made, edges, parts, pair, copies],
    )
    final = call(
        last_kernel,
        given,
        hbm,
        pltpu.HBM(psi_cur.shape, F32),
        SIDES * mac,
        blocks.size,
        [columns, kept, pltpu.VMEM(psi_cur.shape, F32), parts, copies],
    )

    field, inner, outer, send = first(counts, place(radial_terms), place(coriolis), psi_cur, blocks)
    prev = psi_prev
    for iteration in range(STEPS):
        ends = iteration + 1 == STEPS
        got = exchange(send)
        outer = swapped(outer, "hel", 1)
        inner = swapped(inner, "hel", 0)
        rest = local(iteration > 0)(
            counts, prev, radial_terms, kinetic, cent, damp, energies, rotation, coriolis, field, blocks
        )
        if ends:
            rest, before = rest
        back = exchange(route(offsets, got, rest, inner, outer))
        given = (counts, radial_terms, cent, damp, coriolis, back, rest, inner, outer, blocks)
        if ends:
            return before, final(*given)
        prev = field
        field, inner, outer, send = middle(*given)


def solution(mesh):
    in_specs = (
        P("hel", "chan", None),
        P("hel", "chan", None),
        P("hel", "chan", None, None, None, None),
        P(),
        P("hel", "chan"),
        P("hel", "chan"),
        P("hel", "chan"),
        P("hel"),
        P("hel", None),
    )
    out_specs = (P("hel", "chan", None), P("hel", "chan", None))
    return jax.shard_map(body, mesh=mesh, in_specs=in_specs, out_specs=out_specs, check_vma=False)
```

```python
import functools

import jax
import jax.numpy as jnp
import numpy as np
from jax import lax
from jax.experimental import pallas as pl
from jax.experimental.pallas import tpu as pltpu
from jax.sharding import PartitionSpec as P

STEPS = 2
BF = jnp.bfloat16
F32 = jnp.float32
VMEM_LIMIT = 24 * 1024 * 1024
AHEAD = 3
SIDES = 7


def kinetic_matrix(points):
    n = points + 1
    i = np.arange(1, n, dtype=np.float64)[:, None]
    k = i.T
    gap = np.where(i == k, 1.0, i - k)
    parity = 1.0 - 2.0 * (np.abs(i - k) % 2)
    off = parity * (1.0 / np.sin(np.pi * gap / (2 * n)) ** 2 - 1.0 / np.sin(np.pi * (i + k) / (2 * n)) ** 2)
    diagonal = (2.0 * n * n + 1.0) / 3.0 - 1.0 / np.sin(np.pi * i / n) ** 2
    return (np.where(i == k, diagonal, off) * (0.25 / (n * n))).astype(np.float32)


def radial_profiles(points, width):
    r = np.arange(points, dtype=np.float64)
    centrifugal = 0.1 / (1.0 + 8.0 * r / points) ** 2
    damping = np.exp(-0.002 * np.maximum(r - 3 * points // 4, 0.0) ** 2)
    spread = lambda v: np.ascontiguousarray(np.broadcast_to(v.astype(np.float32)[:, None], (points, width)))
    return spread(centrifugal), spread(damping)


def dot_nn(a, b):
    return lax.dot_general(a, b, (((1,), (0,)), ((), ())), preferred_element_type=F32)


def dot_nt(a, b):
    return lax.dot_general(a, b, (((1,), (1,)), ((), ())), preferred_element_type=F32)


def active_row(counts_ref, h, width):
    channel = lax.axis_index("chan") * width + lax.broadcasted_iota(jnp.int32, (1, width), 1)
    return (channel < counts_ref[h]).astype(F32)


def radial_columns(radial_ref, columns_ref):
    columns = radial_ref[...].T
    for l in range(columns.shape[1]):
        columns_ref[l] = jnp.broadcast_to(columns[:, l : l + 1], columns_ref.shape[1:])


def weight(wide, columns):
    return jnp.concatenate([(wide * columns[l]).astype(BF) for l in range(columns.shape[0])], axis=1)


def interleave(a, b, count):
    pieces = (count, -1, a.shape[1])
    return jnp.concatenate([a.reshape(pieces), b.reshape(pieces)], axis=1).astype(BF)


def emit_products(field, blocks_ref, columns, send_ref, arrived=None):
    width = field.shape[1]
    count, rows = send_ref.shape[:2]
    pair = rows // 4
    wide = field.astype(BF).astype(F32)
    weighted = jnp.concatenate([(wide * columns[l]).astype(BF) for l in range(columns.shape[0])], axis=1)
    if arrived is not None:
        arrived()
    send_ref[:, :pair, :] = interleave(wide, dot_nn(weighted, blocks_ref[0].reshape(-1, width)), count)
    for p in range(1, 4):
        rhs = [blocks_ref[j].reshape(-1, width) for j in (2 * p - 1, 2 * p)]
        out = dot_nn(weighted, jnp.concatenate(rhs, axis=1))
        send_ref[:, p * pair : (p + 1) * pair, :] = interleave(out[:, :width], out[:, width:], count)


def fetch(blocks_ref, kept_ref, sem, skip=0):
    arrived = [None] * skip
    for h in range(skip, blocks_ref.shape[0]):
        copy = pltpu.make_async_copy(blocks_ref.at[h, 0, pl.ds(1, SIDES)], kept_ref.at[h], sem.at[h])
        copy.start()
        arrived.append(copy.wait)
    return arrived


def odd_group():
    return lax.rem(lax.axis_index("hel"), 2) == 1


def emit_edges(fields_ref, cor_ref, edge_ref, inner_ref, outer_ref, sem):
    last = cor_ref.shape[0] - 1
    up = (fields_ref[last] * cor_ref[last : last + 1, :]).astype(BF)
    down = fields_ref[0].astype(BF)
    edge_ref[0] = jnp.where(odd_group(), down, up)
    edge_ref[1] = jnp.where(odd_group(), up, down)
    copies = [pltpu.make_async_copy(edge_ref.at[k], ref, sem.at[k]) for k, ref in enumerate((inner_ref, outer_ref))]
    for copy in copies:
        copy.start()
    return copies


def copy_out(h, made_ref, send_ref, sem):
    rows = made_ref.shape[2]
    copy = pltpu.make_async_copy(made_ref.at[h], send_ref.at[:, pl.ds(h * rows, rows), :], sem.at[h])
    copy.start()
    return copy


def first_kernel(
    counts_ref, radial_hbm, cor_hbm, psi_ref, blocks_ref, field_ref, inner_ref, outer_ref, send_ref,
    here_ref, radial_ref, cor_ref, columns_ref, kept_ref, made_ref, edge_ref, small_sem, psi_sem, block_sem, edge_sem, send_sem,
):
    helicities, _, width = field_ref.shape
    psi = [pltpu.make_async_copy(psi_ref.at[h], here_ref.at[h], psi_sem.at[h]) for h in range(helicities)]
    small = [
        pltpu.make_async_copy(radial_hbm, radial_ref, small_sem.at[0]),
        pltpu.make_async_copy(cor_hbm, cor_ref, small_sem.at[1]),
    ]
    for copy in small + psi:
        copy.start()
    arrived = fetch(blocks_ref, kept_ref, block_sem)
    for copy in small:
        copy.wait()
    radial_columns(radial_ref, columns_ref)
    sent = []
    for h in range(helicities):
        psi[h].wait()
        field = here_ref[h].T * active_row(counts_ref, h, width)
        field_ref[h] = field
        if h + 1 == field_ref.shape[0]:
            sent += emit_edges(field_ref, cor_ref, edge_ref, inner_ref, outer_ref, edge_sem)
        emit_products(field, kept_ref.at[h], columns_ref, made_ref.at[h], arrived[h])
        sent.append(copy_out(h, made_ref, send_ref, send_sem))
    for copy in sent:
        copy.wait()


def route_kernel(offsets_ref, got_ref, *refs):
    send_ref, wide_ref = refs[-2:]
    count = got_ref.shape[0]
    helicities = offsets_ref.shape[0]
    rows = got_ref.shape[1] // helicities
    piece = rows // (1 + SIDES)
    for h in range(helicities):
        mine = slice(h * rows, (h + 1) * rows)

        def widen(i, carry):
            for u in range(4):
                wide = got_ref[4 * i + u, mine, :].astype(F32)
                wide_ref[4 * i + u] = wide
                wide_ref[4 * i + u + count] = wide
            return carry

        lax.fori_loop(0, count // 4, widen, 0)
        ahead = [wide_ref.at[pl.ds(offsets_ref[h, j], count)] for j in range(SIDES)]
        behind = [wide_ref.at[pl.ds(count - offsets_ref[h, j], count)] for j in range(SIDES)]
        for d in range(count):
            out = [ref[d, :piece, :] for ref in ahead]
            terms = [ref[d, (1 + j) * piece : (2 + j) * piece, :] for j, ref in enumerate(behind)]
            while len(terms) > 1:
                terms = [sum(terms[k + 1 : k + 2], terms[k]) for k in range(0, len(terms), 2)]
            send_ref[d, mine, :] = jnp.concatenate(out + terms, axis=0).astype(BF)


def forward(sources, blocks, columns, total, arrived=None):
    points, width = total.shape
    terms = blocks[0].shape[0]
    sources = jnp.concatenate(sources, axis=1)
    if arrived is not None:
        arrived()
    for l in range(0, terms, 2):
        rhs = jnp.concatenate([jnp.concatenate([b[l + u] for b in blocks], axis=1) for u in range(2)], axis=0)
        out = dot_nt(sources, rhs)
        for u in range(2):
            total = total + columns[l + u] * out[:, u * width : (u + 1) * width]
    return total


def local_kernel(
    final, counts_ref, prev_ref, radial_ref, kin_ref, cent_ref, damp_ref, e_ref, rot_ref, cor_ref, field_ref, blocks_ref, all_blocks_ref, out_ref, columns, *refs
):
    helicities, points, width = field_ref.shape
    terms = blocks_ref.shape[3]
    cent = cent_ref[...]
    damp = damp_ref[...]
    ahead_sem = refs[-1]
    ahead = [
        pltpu.make_async_copy(all_blocks_ref.at[h, 0, pl.ds(1, SIDES)], refs[h], ahead_sem.at[h]) for h in range(AHEAD)
    ]
    for copy in ahead:
        copy.start()
    radial_columns(radial_ref, columns)
    for h in range(helicities):
        mask = active_row(counts_ref, h, width)
        field = field_ref[h]
        half = field.astype(BF)
        total = lax.dot_general(
            kin_ref[...], field, (((1,), (0,)), ((), ())), precision=lax.Precision.HIGHEST, preferred_element_type=F32
        )
        for l in range(terms):
            total = total + columns[l] * dot_nn(half, blocks_ref[h, 0, 0, l])
        total = forward([half], [blocks_ref.at[h, 0, 0]], columns, total)
        total = total + (e_ref[h : h + 1, :] + cent * rot_ref[h : h + 1, :]) * field
        if h + 1 < helicities:
            total = total - cent * (cor_ref[h : h + 1, :] * field_ref[h + 1])
        if h > 0:
            total = total - cent * (cor_ref[h - 1 : h, :] * field_ref[h - 1])
        previous = prev_ref[h] if final else prev_ref[h].T * mask
        out_ref[h] = damp * (2.0 * (mask * total) - damp * previous)
        if final:
            refs[AHEAD][h] = field.T
    for copy in ahead:
        copy.wait()


def renew(h, got_ref, counts_ref, local_ref, columns, cent_ref, damp_ref, cor_ref, inner_ref, outer_ref, kept_ref, arrived):
    helicities, points, width = local_ref.shape
    rows = got_ref.shape[1] // helicities
    pair = rows // 4
    slots = []
    for p in range(4):
        both = got_ref[:, h * rows + p * pair : h * rows + (p + 1) * pair, :].astype(F32)
        slots += [both[:, : pair // 2].reshape(points, width), both[:, pair // 2 :].reshape(points, width)]
    total = slots[-1]
    if h == 0:
        below = jnp.where(odd_group(), inner_ref[...], outer_ref[...])
        total = total - cent_ref[...] * below.astype(F32)
    if h == helicities - 1:
        above = jnp.where(odd_group(), outer_ref[...], inner_ref[...])
        total = total - cent_ref[...] * (above.astype(F32) * cor_ref[h : h + 1, :])
    sources = [slot.astype(BF) for slot in slots[:-1]]
    total = forward(sources, [kept_ref.at[j] for j in range(SIDES)], columns, total, arrived[h])
    return local_ref[h] + 2.0 * damp_ref[...] * (active_row(counts_ref, h, width) * total)


def middle_kernel(
    counts_ref, columns, cent_ref, damp_ref, cor_ref, got_ref, local_ref, inner_got, outer_got, *refs
):
    blocks_ref, field_ref, inner_ref, outer_ref, send_ref, kept_ref, made_ref, edge_ref, block_sem, edge_sem, send_sem = refs[
        AHEAD:
    ]
    arrived = fetch(blocks_ref, kept_ref, block_sem, AHEAD)
    mine = list(refs[:AHEAD]) + [kept_ref.at[h] for h in range(AHEAD, local_ref.shape[0])]
    sent = []
    for h in range(local_ref.shape[0]):
        field = renew(
            h, got_ref, counts_ref, local_ref, columns, cent_ref, damp_ref, cor_ref, inner_got, outer_got, mine[h], arrived
        )
        field_ref[h] = field
        if h + 1 == field_ref.shape[0]:
            sent += emit_edges(field_ref, cor_ref, edge_ref, inner_ref, outer_ref, edge_sem)
        emit_products(field, mine[h], columns, made_ref.at[h])
        sent.append(copy_out(h, made_ref, send_ref, send_sem))
    for copy in sent:
        copy.wait()


def last_kernel(
    counts_ref, columns, cent_ref, damp_ref, cor_ref, got_ref, local_ref, inner_got, outer_got, *refs
):
    blocks_ref, out_ref, kept_ref, made_ref, block_sem, sem = refs[AHEAD:]
    arrived = fetch(blocks_ref, kept_ref, block_sem, AHEAD)
    mine = list(refs[:AHEAD]) + [kept_ref.at[h] for h in range(AHEAD, local_ref.shape[0])]
    sent = []
    for h in range(local_ref.shape[0]):
        field = renew(
            h, got_ref, counts_ref, local_ref, columns, cent_ref, damp_ref, cor_ref, inner_got, outer_got, mine[h], arrived
        )
        made_ref[h] = field.T
        copy = pltpu.make_async_copy(made_ref.at[h], out_ref.at[h], sem.at[h])
        copy.start()
        sent.append(copy)
    for copy in sent:
        copy.wait()


def swapped(x, axis, first):
    peers = lax.axis_size(axis)
    pairs = [(i, i + 1) for i in range(first, peers - 1, 2)]
    return lax.ppermute(x, axis, pairs + [(j, i) for i, j in pairs])


def exchange(x):
    return lax.all_to_all(x, "chan", 0, 0, tiled=True)


def body(psi_prev, psi_cur, blocks, radial_terms, energies, rotation, coriolis, counts, offsets):
    helicities, width, points = psi_cur.shape
    count = lax.axis_size("chan")
    terms = blocks.shape[3]
    rows = (1 + SIDES) * points // count
    assert blocks.shape[2] == offsets.shape[1] + 1 == SIDES + 1
    kinetic = jnp.asarray(kinetic_matrix(points))
    cent, damp = (jnp.asarray(v) for v in radial_profiles(points, width))

    smem = pl.BlockSpec(memory_space=pltpu.SMEM)
    vmem = pl.BlockSpec(memory_space=pltpu.VMEM)
    hbm = pl.BlockSpec(memory_space=pl.ANY)
    whole = lambda a: pl.BlockSpec(a.shape, lambda *_: (0,) * a.ndim)
    place = lambda a: pltpu.with_memory_space_constraint(a, pltpu.HBM)
    psi_cur, psi_prev, blocks, counts, offsets = map(place, (psi_cur, psi_prev, blocks, counts, offsets))

    field_shape = (helicities, points, width)
    field_out = pltpu.VMEM(field_shape, F32)
    parcel_shape = (count, helicities * rows, width)
    parcel_out = pltpu.HBM(parcel_shape, BF)
    edge_out = pltpu.HBM((points, width), BF)
    edges = pltpu.VMEM((2, points, width), BF)
    pair = pltpu.SemaphoreType.DMA((2,))
    columns = pltpu.VMEM((terms, points, width), F32)
    made = pltpu.VMEM((helicities, count, rows, width), BF)
    ahead_out = pltpu.VMEM((SIDES,) + blocks.shape[3:], BF)
    kept = pltpu.VMEM((helicities, SIDES) + blocks.shape[3:], BF)
    copies = pltpu.SemaphoreType.DMA((helicities,))
    diagonal = pl.BlockSpec((helicities, 1, 1) + blocks.shape[3:], lambda *_: (0,) * blocks.ndim)
    mac = 2 * helicities * points * width * width * terms

    def call(kernel, in_specs, out_specs, out_shape, flops, moved, scratch=()):
        return pl.pallas_call(
            kernel,
            grid=(1,),
            in_specs=in_specs,
            out_specs=out_specs,
            out_shape=out_shape,
            scratch_shapes=scratch,
            compiler_params=pltpu.CompilerParams(vmem_limit_bytes=VMEM_LIMIT),
            cost_estimate=pl.CostEstimate(flops=flops, bytes_accessed=moved, transcendentals=0),
        )

    first = call(
        first_kernel,
        [smem, hbm, hbm, hbm, hbm],
        [vmem, hbm, hbm, hbm],
        [field_out, edge_out, edge_out, parcel_out],
        SIDES * mac,
        blocks.size * 2,
        [
            pltpu.VMEM(psi_cur.shape, F32), pltpu.VMEM(radial_terms.shape, F32), pltpu.VMEM(coriolis.shape, F32), columns, kept,
            made, edges, pair, copies, copies, pair, copies,
        ],
    )
    route = call(
        route_kernel,
        [smem, vmem, hbm, hbm, hbm],
        vmem,
        pltpu.VMEM(parcel_shape, BF),
        psi_cur.size * 8,
        psi_cur.size * 4,
        [pltpu.VMEM((2 * count, rows, width), F32)],
    )

    def local(final):
        kernel = functools.partial(local_kernel, final)
        tables = [whole(a) for a in (psi_prev, radial_terms, kinetic, cent, damp, energies, rotation, coriolis)]
        if final:
            tables[0] = vmem
        out_specs = [vmem] * (2 + AHEAD) + [whole(psi_prev)] * final
        out_shape = [field_out, columns] + [ahead_out] * AHEAD + [pltpu.HBM(psi_prev.shape, F32)] * final
        return call(kernel, [smem] + tables + [vmem, diagonal, hbm], out_specs, out_shape, 2 * mac, 4 * psi_cur.size, [copies])

    given = [smem] + [vmem] * (8 + AHEAD) + [hbm]
    middle = call(
        middle_kernel,
        given,
        [vmem, hbm, hbm, hbm],
        [field_out, edge_out, edge_out, parcel_out],
        2 * SIDES * mac,
        blocks.size,
        [kept, made, edges, copies, pair, copies],
    )
    final = call(
        last_kernel,
        given,
        hbm,
        pltpu.HBM(psi_cur.shape, F32),
        SIDES * mac,
        blocks.size,
        [kept, pltpu.VMEM(psi_cur.shape, F32), copies, copies],
    )

    field, inner, outer, send = first(counts, place(radial_terms), place(coriolis), psi_cur, blocks)
    prev = psi_prev
    for iteration in range(STEPS):
        ends = iteration + 1 == STEPS
        got = exchange(send)
        outer = swapped(outer, "hel", 1)
        inner = swapped(inner, "hel", 0)
        rest = local(iteration > 0)(
            counts, prev, radial_terms, kinetic, cent, damp, energies, rotation, coriolis, field, blocks, blocks
        )
        rest, spread, *more = rest
        ahead, before = more[:AHEAD], more[AHEAD:]
        back = exchange(route(offsets, got, rest, inner, outer))
        given = (counts, spread, cent, damp, coriolis, back, rest, inner, outer, *ahead, blocks)
        if ends:
            return before[0], final(*given)
        prev = field
        field, inner, outer, send = middle(*given)


def solution(mesh):
    in_specs = (
        P("hel", "chan", None),
        P("hel", "chan", None),
        P("hel", "chan", None, None, None, None),
        P(),
        P("hel", "chan"),
        P("hel", "chan"),
        P("hel", "chan"),
        P("hel"),
        P("hel", None),
    )
    out_specs = (P("hel", "chan", None), P("hel", "chan", None))
    return jax.shard_map(body, mesh=mesh, in_specs=in_specs, out_specs=out_specs, check_vma=False)
```

```python
import functools

import jax
import jax.numpy as jnp
import numpy as np
from jax import lax
from jax.experimental import pallas as pl
from jax.experimental.pallas import tpu as pltpu
from jax.sharding import PartitionSpec as P

STEPS = 2
BF = jnp.bfloat16
F32 = jnp.float32
VMEM_LIMIT = 24 * 1024 * 1024
AHEAD = 3
SIDES = 7


def kinetic_matrix(points):
    n = points + 1
    i = np.arange(1, n, dtype=np.float64)[:, None]
    k = i.T
    gap = np.where(i == k, 1.0, i - k)
    parity = 1.0 - 2.0 * (np.abs(i - k) % 2)
    off = parity * (1.0 / np.sin(np.pi * gap / (2 * n)) ** 2 - 1.0 / np.sin(np.pi * (i + k) / (2 * n)) ** 2)
    diagonal = (2.0 * n * n + 1.0) / 3.0 - 1.0 / np.sin(np.pi * i / n) ** 2
    return (np.where(i == k, diagonal, off) * (0.25 / (n * n))).astype(np.float32)


def radial_profiles(points, width):
    r = np.arange(points, dtype=np.float64)
    centrifugal = 0.1 / (1.0 + 8.0 * r / points) ** 2
    damping = np.exp(-0.002 * np.maximum(r - 3 * points // 4, 0.0) ** 2)
    spread = lambda v: np.ascontiguousarray(np.broadcast_to(v.astype(np.float32)[:, None], (points, width)))
    return spread(centrifugal), spread(damping)


def dot_nn(a, b):
    return lax.dot_general(a, b, (((1,), (0,)), ((), ())), preferred_element_type=F32)


def dot_nt(a, b):
    return lax.dot_general(a, b, (((1,), (1,)), ((), ())), preferred_element_type=F32)


def active_row(counts_ref, h, width):
    channel = lax.axis_index("chan") * width + lax.broadcasted_iota(jnp.int32, (1, width), 1)
    return (channel < counts_ref[h]).astype(F32)


def radial_columns(radial_ref, columns_ref):
    columns = radial_ref[...].T
    for l in range(columns.shape[1]):
        columns_ref[l] = jnp.broadcast_to(columns[:, l : l + 1], columns_ref.shape[1:])


def weight(wide, columns):
    return jnp.concatenate([(wide * columns[l]).astype(BF) for l in range(columns.shape[0])], axis=1)


def interleave(a, b, count):
    pieces = (count, -1, a.shape[1])
    return jnp.concatenate([a.reshape(pieces), b.reshape(pieces)], axis=1).astype(BF)


def emit_products(field, blocks_ref, columns, send_ref, arrived=None):
    width = field.shape[1]
    count, rows = send_ref.shape[:2]
    pair = rows // 4
    wide = field.astype(BF).astype(F32)
    weighted = jnp.concatenate([(wide * columns[l]).astype(BF) for l in range(columns.shape[0])], axis=1)
    if arrived is not None:
        arrived()
    send_ref[:, :pair, :] = interleave(wide, dot_nn(weighted, blocks_ref[0].reshape(-1, width)), count)
    for p in range(1, 4):
        rhs = [blocks_ref[j].reshape(-1, width) for j in (2 * p - 1, 2 * p)]
        out = dot_nn(weighted, jnp.concatenate(rhs, axis=1))
        send_ref[:, p * pair : (p + 1) * pair, :] = interleave(out[:, :width], out[:, width:], count)


def fetch(blocks_ref, kept_ref, sem, skip=0):
    arrived = [None] * skip
    for h in range(skip, blocks_ref.shape[0]):
        copy = pltpu.make_async_copy(blocks_ref.at[h, 0, pl.ds(1, SIDES)], kept_ref.at[h], sem.at[h])
        copy.start()
        arrived.append(copy.wait)
    return arrived


def odd_group():
    return lax.rem(lax.axis_index("hel"), 2) == 1


def emit_edges(fields_ref, cor_ref, edge_ref, inner_ref, outer_ref, sem):
    last = cor_ref.shape[0] - 1
    up = (fields_ref[last] * cor_ref[last : last + 1, :]).astype(BF)
    down = fields_ref[0].astype(BF)
    edge_ref[0] = jnp.where(odd_group(), down, up)
    edge_ref[1] = jnp.where(odd_group(), up, down)
    copies = [pltpu.make_async_copy(edge_ref.at[k], ref, sem.at[k]) for k, ref in enumerate((inner_ref, outer_ref))]
    for copy in copies:
        copy.start()
    return copies


def copy_out(h, made_ref, send_ref, sem):
    rows = made_ref.shape[2]
    copy = pltpu.make_async_copy(made_ref.at[h], send_ref.at[:, pl.ds(h * rows, rows), :], sem.at[h])
    copy.start()
    return copy


def first_kernel(
    counts_ref, radial_hbm, cor_hbm, psi_ref, blocks_ref, field_ref, inner_ref, outer_ref, send_ref,
    here_ref, radial_ref, cor_ref, columns_ref, kept_ref, made_ref, edge_ref, small_sem, psi_sem, block_sem, edge_sem, send_sem,
):
    helicities, _, width = field_ref.shape
    psi = [pltpu.make_async_copy(psi_ref.at[h], here_ref.at[h], psi_sem.at[h]) for h in range(helicities)]
    small = [
        pltpu.make_async_copy(radial_hbm, radial_ref, small_sem.at[0]),
        pltpu.make_async_copy(cor_hbm, cor_ref, small_sem.at[1]),
    ]
    for copy in small + psi[:1]:
        copy.start()
    arrived = fetch(blocks_ref, kept_ref, block_sem)
    for copy in psi[1:]:
        copy.start()
    for copy in small:
        copy.wait()
    radial_columns(radial_ref, columns_ref)
    sent = []
    for h in range(helicities):
        psi[h].wait()
        field = here_ref[h].T * active_row(counts_ref, h, width)
        field_ref[h] = field
        if h + 1 == field_ref.shape[0]:
            sent += emit_edges(field_ref, cor_ref, edge_ref, inner_ref, outer_ref, edge_sem)
        emit_products(field, kept_ref.at[h], columns_ref, made_ref.at[h], arrived[h])
        sent.append(copy_out(h, made_ref, send_ref, send_sem))
    for copy in sent:
        copy.wait()


def route_kernel(offsets_ref, got_ref, *refs):
    send_ref, wide_ref = refs[-2:]
    count = got_ref.shape[0]
    helicities = offsets_ref.shape[0]
    rows = got_ref.shape[1] // helicities
    piece = rows // (1 + SIDES)
    for h in range(helicities):
        mine = slice(h * rows, (h + 1) * rows)

        def widen(i, carry):
            for u in range(4):
                wide = got_ref[4 * i + u, mine, :].astype(F32)
                wide_ref[4 * i + u] = wide
                wide_ref[4 * i + u + count] = wide
            return carry

        lax.fori_loop(0, count // 4, widen, 0)
        ahead = [wide_ref.at[pl.ds(offsets_ref[h, j], count)] for j in range(SIDES)]
        behind = [wide_ref.at[pl.ds(count - offsets_ref[h, j], count)] for j in range(SIDES)]
        for d in range(count):
            out = [ref[d, :piece, :] for ref in ahead]
            terms = [ref[d, (1 + j) * piece : (2 + j) * piece, :] for j, ref in enumerate(behind)]
            while len(terms) > 1:
                terms = [sum(terms[k + 1 : k + 2], terms[k]) for k in range(0, len(terms), 2)]
            send_ref[d, mine, :] = jnp.concatenate(out + terms, axis=0).astype(BF)


def forward(sources, blocks, columns, total, arrived=None):
    points, width = total.shape
    terms = blocks[0].shape[0]
    sources = jnp.concatenate(sources, axis=1)
    if arrived is not None:
        arrived()
    for l in range(0, terms, 2):
        rhs = jnp.concatenate([jnp.concatenate([b[l + u] for b in blocks], axis=1) for u in range(2)], axis=0)
        out = dot_nt(sources, rhs)
        for u in range(2):
            total = total + columns[l + u] * out[:, u * width : (u + 1) * width]
    return total


def local_kernel(
    final, counts_ref, prev_ref, radial_ref, kin_ref, cent_ref, damp_ref, e_ref, rot_ref, cor_ref, field_ref, blocks_ref, all_blocks_ref, out_ref, columns, *refs
):
    helicities, points, width = field_ref.shape
    terms = blocks_ref.shape[3]
    cent = cent_ref[...]
    damp = damp_ref[...]
    ahead_sem = refs[-1]
    ahead = [
        pltpu.make_async_copy(all_blocks_ref.at[h, 0, pl.ds(1, SIDES)], refs[h], ahead_sem.at[h]) for h in range(AHEAD)
    ]
    for copy in ahead:
        copy.start()
    radial_columns(radial_ref, columns)
    for h in range(helicities):
        mask = active_row(counts_ref, h, width)
        field = field_ref[h]
        half = field.astype(BF)
        total = lax.dot_general(
            kin_ref[...], field, (((1,), (0,)), ((), ())), precision=lax.Precision.HIGHEST, preferred_element_type=F32
        )
        for l in range(terms):
            total = total + columns[l] * dot_nn(half, blocks_ref[h, 0, 0, l])
        total = forward([half], [blocks_ref.at[h, 0, 0]], columns, total)
        total = total + (e_ref[h : h + 1, :] + cent * rot_ref[h : h + 1, :]) * field
        if h + 1 < helicities:
            total = total - cent * (cor_ref[h : h + 1, :] * field_ref[h + 1])
        if h > 0:
            total = total - cent * (cor_ref[h - 1 : h, :] * field_ref[h - 1])
        previous = prev_ref[h] if final else prev_ref[h].T * mask
        out_ref[h] = damp * (2.0 * (mask * total) - damp * previous)
        if final:
            refs[AHEAD][h] = field.T
    for copy in ahead:
        copy.wait()


def renew(h, got_ref, counts_ref, local_ref, columns, cent_ref, damp_ref, cor_ref, inner_ref, outer_ref, kept_ref, arrived):
    helicities, points, width = local_ref.shape
    rows = got_ref.shape[1] // helicities
    pair = rows // 4
    slots = []
    for p in range(4):
        both = got_ref[:, h * rows + p * pair : h * rows + (p + 1) * pair, :].astype(F32)
        slots += [both[:, : pair // 2].reshape(points, width), both[:, pair // 2 :].reshape(points, width)]
    total = slots[-1]
    if h == 0:
        below = jnp.where(odd_group(), inner_ref[...], outer_ref[...])
        total = total - cent_ref[...] * below.astype(F32)
    if h == helicities - 1:
        above = jnp.where(odd_group(), outer_ref[...], inner_ref[...])
        total = total - cent_ref[...] * (above.astype(F32) * cor_ref[h : h + 1, :])
    sources = [slot.astype(BF) for slot in slots[:-1]]
    total = forward(sources, [kept_ref.at[j] for j in range(SIDES)], columns, total, arrived[h])
    return local_ref[h] + 2.0 * damp_ref[...] * (active_row(counts_ref, h, width) * total)


def middle_kernel(
    counts_ref, columns, cent_ref, damp_ref, cor_ref, got_ref, local_ref, inner_got, outer_got, *refs
):
    blocks_ref, field_ref, inner_ref, outer_ref, send_ref, kept_ref, made_ref, edge_ref, block_sem, edge_sem, send_sem = refs[
        AHEAD:
    ]
    arrived = fetch(blocks_ref, kept_ref, block_sem, AHEAD)
    mine = list(refs[:AHEAD]) + [kept_ref.at[h] for h in range(AHEAD, local_ref.shape[0])]
    sent = []
    for h in range(local_ref.shape[0]):
        field = renew(
            h, got_ref, counts_ref, local_ref, columns, cent_ref, damp_ref, cor_ref, inner_got, outer_got, mine[h], arrived
        )
        field_ref[h] = field
        if h + 1 == field_ref.shape[0]:
            sent += emit_edges(field_ref, cor_ref, edge_ref, inner_ref, outer_ref, edge_sem)
        emit_products(field, mine[h], columns, made_ref.at[h])
        sent.append(copy_out(h, made_ref, send_ref, send_sem))
    for copy in sent:
        copy.wait()


def last_kernel(
    counts_ref, columns, cent_ref, damp_ref, cor_ref, got_ref, local_ref, inner_got, outer_got, *refs
):
    blocks_ref, out_ref, kept_ref, made_ref, block_sem, sem = refs[AHEAD:]
    arrived = fetch(blocks_ref, kept_ref, block_sem, AHEAD)
    mine = list(refs[:AHEAD]) + [kept_ref.at[h] for h in range(AHEAD, local_ref.shape[0])]
    sent = []
    for h in range(local_ref.shape[0]):
        field = renew(
            h, got_ref, counts_ref, local_ref, columns, cent_ref, damp_ref, cor_ref, inner_got, outer_got, mine[h], arrived
        )
        made_ref[h] = field.T
        copy = pltpu.make_async_copy(made_ref.at[h], out_ref.at[h], sem.at[h])
        copy.start()
        sent.append(copy)
    for copy in sent:
        copy.wait()


def swapped(x, axis, first):
    peers = lax.axis_size(axis)
    pairs = [(i, i + 1) for i in range(first, peers - 1, 2)]
    return lax.ppermute(x, axis, pairs + [(j, i) for i, j in pairs])


def exchange(x):
    return lax.all_to_all(x, "chan", 0, 0, tiled=True)


def body(psi_prev, psi_cur, blocks, radial_terms, energies, rotation, coriolis, counts, offsets):
    helicities, width, points = psi_cur.shape
    count = lax.axis_size("chan")
    terms = blocks.shape[3]
    rows = (1 + SIDES) * points // count
    assert blocks.shape[2] == offsets.shape[1] + 1 == SIDES + 1
    kinetic = jnp.asarray(kinetic_matrix(points))
    cent, damp = (jnp.asarray(v) for v in radial_profiles(points, width))

    smem = pl.BlockSpec(memory_space=pltpu.SMEM)
    vmem = pl.BlockSpec(memory_space=pltpu.VMEM)
    hbm = pl.BlockSpec(memory_space=pl.ANY)
    whole = lambda a: pl.BlockSpec(a.shape, lambda *_: (0,) * a.ndim)
    place = lambda a: pltpu.with_memory_space_constraint(a, pltpu.HBM)
    psi_cur, psi_prev, blocks, counts, offsets = map(place, (psi_cur, psi_prev, blocks, counts, offsets))

    field_shape = (helicities, points, width)
    field_out = pltpu.VMEM(field_shape, F32)
    parcel_shape = (count, helicities * rows, width)
    parcel_out = pltpu.HBM(parcel_shape, BF)
    edge_out = pltpu.HBM((points, width), BF)
    edges = pltpu.VMEM((2, points, width), BF)
    pair = pltpu.SemaphoreType.DMA((2,))
    columns = pltpu.VMEM((terms, points, width), F32)
    made = pltpu.VMEM((helicities, count, rows, width), BF)
    ahead_out = pltpu.VMEM((SIDES,) + blocks.shape[3:], BF)
    kept = pltpu.VMEM((helicities, SIDES) + blocks.shape[3:], BF)
    copies = pltpu.SemaphoreType.DMA((helicities,))
    diagonal = pl.BlockSpec((helicities, 1, 1) + blocks.shape[3:], lambda *_: (0,) * blocks.ndim)
    mac = 2 * helicities * points * width * width * terms

    def call(kernel, in_specs, out_specs, out_shape, flops, moved, scratch=()):
        return pl.pallas_call(
            kernel,
            grid=(1,),
            in_specs=in_specs,
            out_specs=out_specs,
            out_shape=out_shape,
            scratch_shapes=scratch,
            compiler_params=pltpu.CompilerParams(vmem_limit_bytes=VMEM_LIMIT),
            cost_estimate=pl.CostEstimate(flops=flops, bytes_accessed=moved, transcendentals=0),
        )

    first = call(
        first_kernel,
        [smem, hbm, hbm, hbm, hbm],
        [vmem, hbm, hbm, hbm],
        [field_out, edge_out, edge_out, parcel_out],
        SIDES * mac,
        blocks.size * 2,
        [
            pltpu.VMEM(psi_cur.shape, F32), pltpu.VMEM(radial_terms.shape, F32), pltpu.VMEM(coriolis.shape, F32), columns, kept,
            made, edges, pair, copies, copies, pair, copies,
        ],
    )
    route = call(
        route_kernel,
        [smem, vmem, hbm, hbm, hbm],
        vmem,
        pltpu.VMEM(parcel_shape, BF),
        psi_cur.size * 8,
        psi_cur.size * 4,
        [pltpu.VMEM((2 * count, rows, width), F32)],
    )

    def local(final):
        kernel = functools.partial(local_kernel, final)
        tables = [whole(a) for a in (psi_prev, radial_terms, kinetic, cent, damp, energies, rotation, coriolis)]
        if final:
            tables[0] = vmem
        out_specs = [vmem] * (2 + AHEAD) + [whole(psi_prev)] * final
        out_shape = [field_out, columns] + [ahead_out] * AHEAD + [pltpu.HBM(psi_prev.shape, F32)] * final
        return call(kernel, [smem] + tables + [vmem, diagonal, hbm], out_specs, out_shape, 2 * mac, 4 * psi_cur.size, [copies])

    given = [smem] + [vmem] * (8 + AHEAD) + [hbm]
    middle = call(
        middle_kernel,
        given,
        [vmem, hbm, hbm, hbm],
        [field_out, edge_out, edge_out, parcel_out],
        2 * SIDES * mac,
        blocks.size,
        [kept, made, edges, copies, pair, copies],
    )
    final = call(
        last_kernel,
        given,
        hbm,
        pltpu.HBM(psi_cur.shape, F32),
        SIDES * mac,
        blocks.size,
        [kept, pltpu.VMEM(psi_cur.shape, F32), copies, copies],
    )

    field, inner, outer, send = first(counts, place(radial_terms), place(coriolis), psi_cur, blocks)
    prev = psi_prev
    for iteration in range(STEPS):
        ends = iteration + 1 == STEPS
        got = exchange(send)
        outer = swapped(outer, "hel", 1)
        inner = swapped(inner, "hel", 0)
        rest = local(iteration > 0)(
            counts, prev, radial_terms, kinetic, cent, damp, energies, rotation, coriolis, field, blocks, blocks
        )
        rest, spread, *more = rest
        ahead, before = more[:AHEAD], more[AHEAD:]
        back = exchange(route(offsets, got, rest, inner, outer))
        given = (counts, spread, cent, damp, coriolis, back, rest, inner, outer, *ahead, blocks)
        if ends:
            return before[0], final(*given)
        prev = field
        field, inner, outer, send = middle(*given)


def solution(mesh):
    in_specs = (
        P("hel", "chan", None),
        P("hel", "chan", None),
        P("hel", "chan", None, None, None, None),
        P(),
        P("hel", "chan"),
        P("hel", "chan"),
        P("hel", "chan"),
        P("hel"),
        P("hel", None),
    )
    out_specs = (P("hel", "chan", None), P("hel", "chan", None))
    return jax.shard_map(body, mesh=mesh, in_specs=in_specs, out_specs=out_specs, check_vma=False)
```
